32 devices in a mesh: mom: 2 (over x), en: 16 (over z, y, core).
Axes of the slice: x: 2, y: 2, z: 4, core: 2. Of those that a mesh axis runs over, the one named last changes fastest.
Arguments:
- green: bfloat16 [2, 128, 2, 2, 64, 128], P('mom', 'en'), may hold values from -6 to 6
- pair_index: int32 [2, 4], replicated, may hold values from 0 to 1
- pair_weight: float32 [2, 4], replicated, may hold values from 0.1 to 0.4
- phonon_offset: int32 [4], replicated, may hold values from 1 to 4, as said below
- occupation: float32 [4], replicated, may hold values from 0.2 to 3
- vertex: bfloat16 [4, 8, 64, 64], replicated, may hold values from -0.75 to 0.75
- block_atoms: int32 [2, 2], replicated, may hold values from 0 to 7
Outputs:
- self_energy: bfloat16 [2, 128, 2, 2, 64, 128], P('mom', 'en')
The draws below stay inside these ranges and needn't reach their ends.
Inputs may be any that keep to these rules, and one draw needn't show every extreme that they name: `phonon_offset`: every mode's offset lies in 1 to 4, and some mode's offset is 4.
All inputs are finite; a program needn't handle non-finite values.
Results may differ from the reference program's by a relative error of at most 0.015.
Values may be sent and summed in bfloat16 or wider, within the bound.
A program may use at most 64 MiB of HBM per device.

```python
import math
import jax
import jax.numpy as jnp
from jax import lax

NORB = 64
NMODE = 4
NATOM = 8
NBLK = 2
PAIRS = 4
OFF_MAX = 4
NK = 2
NE = 128


def draw_phonon_offset(key, part):
    first, second = jax.random.split(jax.random.fold_in(key, 7))
    values = jax.random.randint(first, (NMODE,), 1, OFF_MAX + 1)
    chosen = jax.random.randint(second, (), 0, NMODE)
    return jnp.where(jnp.arange(NMODE) == chosen, OFF_MAX, values).astype(jnp.int32)


def with_ends(values, rng, low, top_value):
    longest = values.shape.index(max(values.shape))
    spots = []
    for shift in (0, 1):
        where = [jax.random.randint(jax.random.fold_in(rng, axis), (), 0, length) for axis, length in enumerate(values.shape)]
        where[longest] = (where[longest] + shift) % values.shape[longest]
        spots.append(tuple(where))
    return values.at[spots[0]].set(low).at[spots[1]].set(top_value)


def level_of(rng, extent, cuts, low, high):
    loudness, own = 1.0, jax.random.fold_in(rng, 6)
    for dim, shards_of in cuts:
        draws = jnp.exp(jax.random.uniform(jax.random.fold_in(own, dim), (shards_of,), jnp.float32, low / len(cuts), high / len(cuts)))
        loudness = loudness * jnp.repeat(draws, extent[dim] // shards_of).reshape([-1 if axis == dim else 1 for axis in range(len(extent))])
    return loudness


def gaussian(own_key, dims, scale, bound, cuts=(), kind=jnp.bfloat16):
    result = scale * jax.random.normal(own_key, dims, jnp.float32)
    if cuts:
        result = result * level_of(own_key, dims, cuts, -0.22, 0.18)
    return jnp.clip(result, -bound, bound).astype(kind)


def setup_inputs(seed: int = 0) -> dict:
    seeds = jax.random.split(jax.random.key(seed), 8)
    return {
        "green": gaussian(seeds[0], (NK, NE, NBLK, 2, NORB, 2 * NORB), 1.0, 6.0, ((0, 2), (1, 16))),
        "pair_index": with_ends(jax.random.randint(seeds[1], (NK, PAIRS), 0, NK), jax.random.fold_in(seeds[1], 1), 0, NK - 1).astype(jnp.int32),
        "pair_weight": jnp.clip(jax.random.uniform(seeds[2], (NK, PAIRS), jnp.float32, 0.1, 0.4), 0.1, 0.4),
        "phonon_offset": draw_phonon_offset(jax.random.fold_in(seeds[7], 71), 0),
        "occupation": jnp.clip(jnp.exp(jax.random.uniform(seeds[4], (NMODE,), jnp.float32, math.log(0.2), math.log(3.0))), 0.2, 3.0),
        "vertex": gaussian(seeds[5], (NMODE, NATOM, NORB, NORB), NORB ** -0.5, 0.75),
        "block_atoms": with_ends(jax.random.randint(seeds[6], (NBLK, 2), 0, NATOM), jax.random.fold_in(seeds[6], 1), 0, NATOM - 1).astype(jnp.int32),
    }


def reference(green, pair_index, pair_weight, phonon_offset, occupation, vertex, block_atoms):
    paired = jnp.zeros(green.shape, jnp.float32)
    for j in range(PAIRS):
        picked = green[pair_index[:, j].astype(jnp.int32)].astype(jnp.float32)
        paired = paired + pair_weight[:, j][:, None, None, None, None, None] * picked
    paired = paired.astype(jnp.bfloat16)
    padding = jnp.zeros((NK, OFF_MAX) + green.shape[2:], jnp.bfloat16)
    extended = jnp.concatenate([padding, paired, padding], axis=1)
    total = jnp.zeros((NK, NE, NBLK, 2, NORB, 2, NORB), jnp.float32)
    for m in range(NMODE):
        shift_by = phonon_offset[m].astype(jnp.int32)
        plus = lax.dynamic_slice_in_dim(extended, OFF_MAX + shift_by, NE, 1).astype(jnp.float32)
        minus = lax.dynamic_slice_in_dim(extended, OFF_MAX - shift_by, NE, 1).astype(jnp.float32)
        bose = occupation[m]
        lesser = (bose + 1.0) * plus[:, :, :, 0] + bose * minus[:, :, :, 0]
        greater = bose * plus[:, :, :, 1] + (bose + 1.0) * minus[:, :, :, 1]
        source = jnp.stack([lesser, greater], axis=3).astype(jnp.bfloat16)
        left_block = vertex[m][block_atoms[:, 0].astype(jnp.int32)].astype(jnp.float32)
        right_block = vertex[m][block_atoms[:, 1].astype(jnp.int32)].astype(jnp.float32)
        half = jnp.einsum("bij,kebtjc->kebtic", left_block, source.astype(jnp.float32)).astype(jnp.bfloat16)
        parts = half.reshape((NK, NE, NBLK, 2, NORB, 2, NORB)).astype(jnp.float32)
        total = total + jnp.einsum("kebtipj,blj->kebtipl", parts, right_block)
    return total.reshape(green.shape).astype(jnp.bfloat16)
```

```python
import functools

import jax
import jax.numpy as jnp
from jax import lax
from jax.experimental import pallas as pl
from jax.experimental.pallas import tpu as pltpu
from jax.sharding import PartitionSpec as P

OFF_MAX = 4
MESH = pl.DeviceIdType.MESH


def kernel(
    n_mom,
    n_en,
    green,
    vertex,
    pair_index,
    pair_weight,
    offset,
    occupation,
    atoms,
    out,
    own,
    got,
    verts,
    left_w,
    right_w,
    result,
    x_send,
    x_recv,
    h_send,
    h_recv,
    local_sem,
    out_sem,
    *ext,
):
    e_local, blocks = green.shape[1], green.shape[2]
    norb = green.shape[4]
    modes = vertex.shape[0]
    pairs = pair_index.shape[1]
    chunks = 2 * blocks
    half = e_local // 2
    me_k, me_e = lax.axis_index("mom"), lax.axis_index("en")
    odd = lax.rem(me_e, 2)
    starts = (odd * half, half - odd * half)
    peers = (me_e - 1 + 2 * odd, me_e + 1 - 2 * odd)
    there = tuple(jnp.logical_and(p >= 0, p < n_en) for p in peers)
    low_edge, high_edge = OFF_MAX, e_local
    send_from = (low_edge + odd * (high_edge - low_edge), high_edge - odd * (high_edge - low_edge))
    mine_at = (odd * (OFF_MAX + e_local), (1 - odd) * (OFF_MAX + e_local))
    peer_at = ((1 - odd) * (OFF_MAX + e_local), odd * (OFF_MAX + e_local))

    barrier = pltpu.get_barrier_semaphore()
    for d in range(1, n_mom):
        pl.semaphore_signal(
            barrier, inc=1, device_id={"mom": lax.rem(me_k + d, n_mom)}, device_id_type=MESH
        )
    for ph in range(2):

        @pl.when(there[ph])
        def _():
            pl.semaphore_signal(barrier, inc=1, device_id={"en": peers[ph]}, device_id_type=MESH)

    met = sum((t.astype(jnp.int32) for t in there), jnp.int32(n_mom - 1))
    pl.semaphore_wait(barrier, met)

    def cross(ph, c, d):
        b, t = divmod(c, 2)
        es = pl.ds(starts[ph], half)
        return pltpu.make_async_remote_copy(
            src_ref=green.at[0, es, b, t],
            dst_ref=got.at[d - 1, c, es],
            send_sem=x_send.at[ph, c, d - 1],
            recv_sem=x_recv.at[ph, c, d - 1],
            device_id={"mom": lax.rem(me_k + d, n_mom)},
            device_id_type=MESH,
        )

    def halo(ph, c):
        return pltpu.make_async_remote_copy(
            src_ref=ext[c].at[pl.ds(send_from[ph], OFF_MAX)],
            dst_ref=ext[c].at[pl.ds(peer_at[ph], OFF_MAX)],
            send_sem=h_send.at[ph, c],
            recv_sem=h_recv.at[ph, c],
            device_id={"en": peers[ph]},
            device_id_type=MESH,
        )

    for ph in range(2):
        for c in range(chunks):
            for d in range(1, n_mom):
                cross(ph, c, d).start()
    get_own = pltpu.make_async_copy(green.at[0], own, local_sem.at[0])
    get_own.start()
    get_verts = pltpu.make_async_copy(vertex, verts, local_sem.at[1])
    get_verts.start()

    def share(q):
        total = jnp.float32(0.0)
        for j in range(pairs):
            total += jnp.where(pair_index[me_k, j] == q, pair_weight[me_k, j], jnp.float32(0.0))
        return total

    shares = [share(lax.rem(me_k - d + n_mom, n_mom)) for d in range(n_mom)]

    for ph in range(2):

        @pl.when(jnp.logical_not(there[ph]))
        def _():
            for c in range(chunks):
                ext[c][pl.ds(mine_at[ph], OFF_MAX)] = jnp.zeros(
                    (OFF_MAX, norb, 2 * norb), jnp.bfloat16
                )

    get_verts.wait()
    none = jnp.zeros((norb, norb), jnp.float32)
    for b in range(blocks):
        for m in range(modes):
            left_w[b, m] = verts[m, atoms[b, 0]]
            turned = verts[m, atoms[b, 1]].astype(jnp.float32).T
            right_w[b, pl.ds(2 * m * norb, norb)] = jnp.concatenate([turned, none], axis=1).astype(
                jnp.bfloat16
            )
            right_w[b, pl.ds((2 * m + 1) * norb, norb)] = jnp.concatenate(
                [none, turned], axis=1
            ).astype(jnp.bfloat16)
    get_own.wait()

    def pair_sum(ph, c):
        b, t = divmod(c, 2)
        es = pl.ds(starts[ph], half)
        total = shares[0] * own[es, b, t].astype(jnp.float32)
        for d in range(1, n_mom):
            cross(ph, c, d).wait_recv()
            total += shares[d] * got[d - 1, c, es].astype(jnp.float32)
        ext[c][pl.ds(OFF_MAX + starts[ph], half)] = total.astype(jnp.bfloat16)

        @pl.when(there[ph])
        def _():
            halo(ph, c).start()

    def store(c):
        b, t = divmod(c, 2)
        return pltpu.make_async_copy(result.at[c], out.at[0, :, b, t], out_sem.at[c])

    def compute(c):
        b, t = divmod(c, 2)
        for ph in range(2):

            @pl.when(there[ph])
            def _():
                halo(ph, c).wait_recv()

        lefts = []
        for m in range(modes):
            w, bose = offset[m], occupation[m]
            up, down = (bose + 1.0, bose) if t == 0 else (bose, bose + 1.0)
            plus = ext[c][pl.ds(OFF_MAX + w, e_local)].astype(jnp.float32)
            minus = ext[c][pl.ds(OFF_MAX - w, e_local)].astype(jnp.float32)
            source = (up * plus + down * minus).astype(jnp.bfloat16)
            wide = jnp.concatenate([source[e] for e in range(e_local)], axis=1)
            lefts.append(
                jnp.dot(left_w[b, m], wide, preferred_element_type=jnp.float32).astype(jnp.bfloat16)
            )
        tall = jnp.concatenate(
            [
                jnp.concatenate([x[:, 2 * norb * e : 2 * norb * (e + 1)] for x in lefts], axis=1)
                for e in range(e_local)
            ],
            axis=0,
        )
        total = jnp.dot(tall, right_w[b], preferred_element_type=jnp.float32)
        result[c] = total.astype(jnp.bfloat16).reshape(e_local, norb, 2 * norb)
        store(c).start()

    for c in range(chunks):
        pair_sum(0, c)
    for c in range(chunks):
        pair_sum(1, c)
        if c > 0:
            compute(c - 1)
    compute(chunks - 1)

    for ph in range(2):
        for c in range(chunks):
            for d in range(1, n_mom):
                cross(ph, c, d).wait_send()

        @pl.when(there[ph])
        def _():
            for c in range(chunks):
                halo(ph, c).wait_send()

    for c in range(chunks):
        store(c).wait()


def local(n_mom, n_en, green, pair_index, pair_weight, offset, occupation, vertex, atoms):
    _, e_local, blocks, _, norb, _ = green.shape
    modes = vertex.shape[0]
    chunks = 2 * blocks
    tile = (norb, 2 * norb)
    slots = max(n_mom - 1, 1)
    bf16 = jnp.bfloat16
    hbm = pl.BlockSpec(memory_space=pl.ANY)
    smem = pl.BlockSpec(memory_space=pltpu.SMEM)
    dma = pltpu.SemaphoreType.DMA
    flops = 2 * e_local * chunks * modes * norb * norb * 4 * norb
    return pl.pallas_call(
        functools.partial(kernel, n_mom, n_en),
        out_shape=jax.ShapeDtypeStruct(green.shape, bf16),
        in_specs=[hbm, hbm, smem, smem, smem, smem, smem],
        out_specs=hbm,
        scratch_shapes=[
            pltpu.VMEM(green.shape[1:], bf16),
            pltpu.VMEM((slots, chunks, e_local) + tile, bf16),
            pltpu.VMEM(vertex.shape, bf16),
            pltpu.VMEM((blocks, modes, norb, norb), bf16),
            pltpu.VMEM((blocks, 2 * modes * norb, 2 * norb), bf16),
            pltpu.VMEM((chunks, e_local) + tile, bf16),
            dma((2, chunks, slots)),
            dma((2, chunks, slots)),
            dma((2, chunks)),
            dma((2, chunks)),
            dma((2,)),
            dma((chunks,)),
        ]
        + [pltpu.VMEM((e_local + 2 * OFF_MAX,) + tile, bf16) for _ in range(chunks)],
        compiler_params=pltpu.CompilerParams(
            collective_id=0, has_side_effects=True, vmem_limit_bytes=60 * 2**20
        ),
        cost_estimate=pl.CostEstimate(
            flops=flops, bytes_accessed=4 * green.size, transcendentals=0
        ),
    )(green, vertex, pair_index, pair_weight, offset, occupation, atoms)


def solution(mesh):
    spec = P("mom", "en", None, None, None, None)
    body = functools.partial(local, mesh.shape["mom"], mesh.shape["en"])
    return jax.shard_map(
        body, mesh=mesh, in_specs=(spec,) + (P(),) * 6, out_specs=spec, check_vma=False
    )
```

```python
import functools

import jax
import jax.numpy as jnp
from jax import lax
from jax.experimental import pallas as pl
from jax.experimental.pallas import tpu as pltpu
from jax.sharding import PartitionSpec as P

OFF_MAX = 4
MESH = pl.DeviceIdType.MESH


def kernel(
    n_mom,
    n_en,
    green,
    vertex,
    pair_index_in,
    pair_weight_in,
    offset_in,
    occupation_in,
    atoms_in,
    out,
    pair_index,
    pair_weight,
    offset,
    occupation,
    atoms,
    own,
    got,
    verts,
    left_w,
    right_w,
    result,
    x_send,
    x_recv,
    h_send,
    h_recv,
    local_sem,
    out_sem,
    *ext,
):
    e_local, blocks = green.shape[1], green.shape[2]
    norb = green.shape[4]
    modes = vertex.shape[0]
    pairs = pair_index_in.shape[1]
    chunks = 2 * blocks
    half = e_local // 2
    me_k, me_e = lax.axis_index("mom"), lax.axis_index("en")
    odd = lax.rem(me_e, 2)
    starts = (odd * half, half - odd * half)
    peers = (me_e - 1 + 2 * odd, me_e + 1 - 2 * odd)
    there = tuple(jnp.logical_and(p >= 0, p < n_en) for p in peers)
    low_edge, high_edge = OFF_MAX, e_local
    send_from = (low_edge + odd * (high_edge - low_edge), high_edge - odd * (high_edge - low_edge))
    mine_at = (odd * (OFF_MAX + e_local), (1 - odd) * (OFF_MAX + e_local))
    peer_at = ((1 - odd) * (OFF_MAX + e_local), odd * (OFF_MAX + e_local))

    barrier = pltpu.get_barrier_semaphore()
    for d in range(1, n_mom):
        pl.semaphore_signal(
            barrier, inc=1, device_id={"mom": lax.rem(me_k + d, n_mom)}, device_id_type=MESH
        )
    for ph in range(2):

        @pl.when(there[ph])
        def _():
            pl.semaphore_signal(barrier, inc=1, device_id={"en": peers[ph]}, device_id_type=MESH)

    met = sum((t.astype(jnp.int32) for t in there), jnp.int32(n_mom - 1))
    pl.semaphore_wait(barrier, met)

    def cross(ph, c, d):
        b, t = divmod(c, 2)
        es = pl.ds(starts[ph], half)
        return pltpu.make_async_remote_copy(
            src_ref=green.at[0, es, b, t],
            dst_ref=got.at[d - 1, c, es],
            send_sem=x_send.at[ph, c, d - 1],
            recv_sem=x_recv.at[ph, c, d - 1],
            device_id={"mom": lax.rem(me_k + d, n_mom)},
            device_id_type=MESH,
        )

    def halo(ph, c):
        return pltpu.make_async_remote_copy(
            src_ref=ext[c].at[pl.ds(send_from[ph], OFF_MAX)],
            dst_ref=ext[c].at[pl.ds(peer_at[ph], OFF_MAX)],
            send_sem=h_send.at[ph, c],
            recv_sem=h_recv.at[ph, c],
            device_id={"en": peers[ph]},
            device_id_type=MESH,
        )

    for ph in range(2):
        for c in range(chunks):
            for d in range(1, n_mom):
                cross(ph, c, d).start()
    smalls = (
        (pair_index_in, pair_index),
        (pair_weight_in, pair_weight),
        (offset_in, offset),
        (occupation_in, occupation),
        (atoms_in, atoms),
    )
    gets = [
        pltpu.make_async_copy(src, dst, local_sem.at[2 + i]) for i, (src, dst) in enumerate(smalls)
    ]
    for get in gets:
        get.start()
    get_own = pltpu.make_async_copy(green.at[0], own, local_sem.at[0])
    get_own.start()
    get_verts = pltpu.make_async_copy(vertex, verts, local_sem.at[1])
    get_verts.start()

    for get in gets:
        get.wait()

    def share(q):
        total = jnp.float32(0.0)
        for j in range(pairs):
            total += jnp.where(pair_index[me_k, j] == q, pair_weight[me_k, j], jnp.float32(0.0))
        return total

    shares = [share(lax.rem(me_k - d + n_mom, n_mom)) for d in range(n_mom)]

    for ph in range(2):

        @pl.when(jnp.logical_not(there[ph]))
        def _():
            for c in range(chunks):
                ext[c][pl.ds(mine_at[ph], OFF_MAX)] = jnp.zeros(
                    (OFF_MAX, norb, 2 * norb), jnp.bfloat16
                )

    get_verts.wait()
    none = jnp.zeros((norb, norb), jnp.float32)
    for b in range(blocks):
        for m in range(modes):
            left_w[b, m] = verts[m, atoms[b, 0]]
            turned = verts[m, atoms[b, 1]].astype(jnp.float32).T
            right_w[b, pl.ds(2 * m * norb, norb)] = jnp.concatenate([turned, none], axis=1).astype(
                jnp.bfloat16
            )
            right_w[b, pl.ds((2 * m + 1) * norb, norb)] = jnp.concatenate(
                [none, turned], axis=1
            ).astype(jnp.bfloat16)
    get_own.wait()

    def pair_sum(ph, c):
        b, t = divmod(c, 2)
        es = pl.ds(starts[ph], half)
        total = shares[0] * own[es, b, t].astype(jnp.float32)
        for d in range(1, n_mom):
            cross(ph, c, d).wait_recv()
            total += shares[d] * got[d - 1, c, es].astype(jnp.float32)
        ext[c][pl.ds(OFF_MAX + starts[ph], half)] = total.astype(jnp.bfloat16)

        @pl.when(there[ph])
        def _():
            halo(ph, c).start()

    def store(c):
        b, t = divmod(c, 2)
        return pltpu.make_async_copy(result.at[c], out.at[0, :, b, t], out_sem.at[c])

    def compute(c):
        b, t = divmod(c, 2)
        for ph in range(2):

            @pl.when(there[ph])
            def _():
                halo(ph, c).wait_recv()

        lefts = []
        for m in range(modes):
            w, bose = offset[m], occupation[m]
            up, down = (bose + 1.0, bose) if t == 0 else (bose, bose + 1.0)
            plus = ext[c][pl.ds(OFF_MAX + w, e_local)].astype(jnp.float32)
            minus = ext[c][pl.ds(OFF_MAX - w, e_local)].astype(jnp.float32)
            source = (up * plus + down * minus).astype(jnp.bfloat16)
            wide = jnp.concatenate([source[e] for e in range(e_local)], axis=1)
            lefts.append(
                jnp.dot(left_w[b, m], wide, preferred_element_type=jnp.float32).astype(jnp.bfloat16)
            )
        tall = jnp.concatenate(
            [
                jnp.concatenate([x[:, 2 * norb * e : 2 * norb * (e + 1)] for x in lefts], axis=1)
                for e in range(e_local)
            ],
            axis=0,
        )
        total = jnp.dot(tall, right_w[b], preferred_element_type=jnp.float32)
        result[c] = total.astype(jnp.bfloat16).reshape(e_local, norb, 2 * norb)
        store(c).start()

    for c in range(chunks):
        pair_sum(0, c)
    for c in range(chunks):
        pair_sum(1, c)
        if c > 0:
            compute(c - 1)
    compute(chunks - 1)

    for ph in range(2):
        for c in range(chunks):
            for d in range(1, n_mom):
                cross(ph, c, d).wait_send()

        @pl.when(there[ph])
        def _():
            for c in range(chunks):
                halo(ph, c).wait_send()

    for c in range(chunks):
        store(c).wait()


def local(n_mom, n_en, green, pair_index, pair_weight, offset, occupation, vertex, atoms):
    _, e_local, blocks, _, norb, _ = green.shape
    modes = vertex.shape[0]
    chunks = 2 * blocks
    tile = (norb, 2 * norb)
    slots = max(n_mom - 1, 1)
    bf16 = jnp.bfloat16
    hbm = pl.BlockSpec(memory_space=pl.ANY)
    small = (pair_index, pair_weight, offset, occupation, atoms)
    dma = pltpu.SemaphoreType.DMA
    flops = 2 * e_local * chunks * modes * norb * norb * 4 * norb
    return pl.pallas_call(
        functools.partial(kernel, n_mom, n_en),
        out_shape=jax.ShapeDtypeStruct(green.shape, bf16),
        in_specs=[hbm] * 7,
        out_specs=hbm,
        scratch_shapes=[pltpu.SMEM(x.shape, x.dtype) for x in small]
        + [
            pltpu.VMEM(green.shape[1:], bf16),
            pltpu.VMEM((slots, chunks, e_local) + tile, bf16),
            pltpu.VMEM(vertex.shape, bf16),
            pltpu.VMEM((blocks, modes, norb, norb), bf16),
            pltpu.VMEM((blocks, 2 * modes * norb, 2 * norb), bf16),
            pltpu.VMEM((chunks, e_local) + tile, bf16),
            dma((2, chunks, slots)),
            dma((2, chunks, slots)),
            dma((2, chunks)),
            dma((2, chunks)),
            dma((2 + len(small),)),
            dma((chunks,)),
        ]
        + [pltpu.VMEM((e_local + 2 * OFF_MAX,) + tile, bf16) for _ in range(chunks)],
        compiler_params=pltpu.CompilerParams(
            collective_id=0, has_side_effects=True, vmem_limit_bytes=60 * 2**20
        ),
        cost_estimate=pl.CostEstimate(
            flops=flops, bytes_accessed=4 * green.size, transcendentals=0
        ),
    )(green, vertex, pair_index, pair_weight, offset, occupation, atoms)


def solution(mesh):
    spec = P("mom", "en", None, None, None, None)
    body = functools.partial(local, mesh.shape["mom"], mesh.shape["en"])
    return jax.shard_map(
        body, mesh=mesh, in_specs=(spec,) + (P(),) * 6, out_specs=spec, check_vma=False
    )
```

```python
import functools

import jax
import jax.numpy as jnp
from jax import lax
from jax.experimental import pallas as pl
from jax.experimental.pallas import tpu as pltpu
from jax.sharding import PartitionSpec as P

OFF_MAX = 4
MESH = pl.DeviceIdType.MESH


def kernel(
    n_mom,
    n_en,
    green,
    vertex,
    pair_index_in,
    pair_weight_in,
    offset_in,
    occupation_in,
    atoms_in,
    out,
    pair_index,
    pair_weight,
    offset,
    occupation,
    atoms,
    own,
    got,
    verts,
    left_w,
    right_w,
    result,
    x_send,
    x_recv,
    h_send,
    h_recv,
    local_sem,
    out_sem,
    *ext,
):
    e_local, blocks = green.shape[1], green.shape[2]
    norb = green.shape[4]
    modes = vertex.shape[0]
    pairs = pair_index_in.shape[1]
    chunks = 2 * blocks
    half = e_local // 2
    me_k, me_e = lax.axis_index("mom"), lax.axis_index("en")
    odd = lax.rem(me_e, 2)
    starts = (odd * half, half - odd * half)
    peers = (me_e - 1 + 2 * odd, me_e + 1 - 2 * odd)
    there = tuple(jnp.logical_and(p >= 0, p < n_en) for p in peers)
    low_edge, high_edge = OFF_MAX, e_local
    send_from = (low_edge + odd * (high_edge - low_edge), high_edge - odd * (high_edge - low_edge))
    mine_at = (odd * (OFF_MAX + e_local), (1 - odd) * (OFF_MAX + e_local))
    peer_at = ((1 - odd) * (OFF_MAX + e_local), odd * (OFF_MAX + e_local))

    barrier = pltpu.get_barrier_semaphore()
    for d in range(1, n_mom):
        pl.semaphore_signal(
            barrier, inc=1, device_id={"mom": lax.rem(me_k + d, n_mom)}, device_id_type=MESH
        )
    for ph in range(2):

        @pl.when(there[ph])
        def _():
            pl.semaphore_signal(barrier, inc=1, device_id={"en": peers[ph]}, device_id_type=MESH)

    met = sum((t.astype(jnp.int32) for t in there), jnp.int32(n_mom - 1))
    pl.semaphore_wait(barrier, met)

    def cross(ph, c, d):
        b, t = divmod(c, 2)
        es = pl.ds(starts[ph], half)
        return pltpu.make_async_remote_copy(
            src_ref=green.at[0, es, b, t],
            dst_ref=got.at[d - 1, c, es],
            send_sem=x_send.at[ph, c, d - 1],
            recv_sem=x_recv.at[ph, c, d - 1],
            device_id={"mom": lax.rem(me_k + d, n_mom)},
            device_id_type=MESH,
        )

    def halo(ph, c):
        return pltpu.make_async_remote_copy(
            src_ref=ext[c].at[pl.ds(send_from[ph], OFF_MAX)],
            dst_ref=ext[c].at[pl.ds(peer_at[ph], OFF_MAX)],
            send_sem=h_send.at[ph, c],
            recv_sem=h_recv.at[ph, c],
            device_id={"en": peers[ph]},
            device_id_type=MESH,
        )

    for ph in range(2):
        for c in range(chunks):
            for d in range(1, n_mom):
                cross(ph, c, d).start()
    smalls = (
        (pair_index_in, pair_index),
        (pair_weight_in, pair_weight),
        (offset_in, offset),
        (occupation_in, occupation),
        (atoms_in, atoms),
    )
    gets = [
        pltpu.make_async_copy(src, dst, local_sem.at[2 + i]) for i, (src, dst) in enumerate(smalls)
    ]
    for get in gets:
        get.start()
    get_own = pltpu.make_async_copy(green.at[0], own, local_sem.at[0])
    get_own.start()
    get_verts = pltpu.make_async_copy(vertex, verts, local_sem.at[1])
    get_verts.start()

    for get in gets:
        get.wait()

    def share(q):
        total = jnp.float32(0.0)
        for j in range(pairs):
            total += jnp.where(pair_index[me_k, j] == q, pair_weight[me_k, j], jnp.float32(0.0))
        return total

    shares = [share(lax.rem(me_k - d + n_mom, n_mom)) for d in range(n_mom)]

    for ph in range(2):

        @pl.when(jnp.logical_not(there[ph]))
        def _():
            for c in range(chunks):
                ext[c][pl.ds(mine_at[ph], OFF_MAX)] = jnp.zeros(
                    (OFF_MAX, norb, 2 * norb), jnp.bfloat16
                )

    get_verts.wait()
    none = jnp.zeros((norb, norb), jnp.float32)
    for b in range(blocks):
        for m in range(modes):
            left_w[b, m] = verts[m, atoms[b, 0]]
            turned = verts[m, atoms[b, 1]].astype(jnp.float32).T
            right_w[b, pl.ds(2 * m * norb, norb)] = jnp.concatenate([turned, none], axis=1).astype(
                jnp.bfloat16
            )
            right_w[b, pl.ds((2 * m + 1) * norb, norb)] = jnp.concatenate(
                [none, turned], axis=1
            ).astype(jnp.bfloat16)
    get_own.wait()

    def pair_sum(ph, c):
        b, t = divmod(c, 2)
        es = pl.ds(starts[ph], half)
        total = shares[0] * own[es, b, t].astype(jnp.float32)
        for d in range(1, n_mom):
            cross(ph, c, d).wait_recv()
            total += shares[d] * got[d - 1, c, es].astype(jnp.float32)
        ext[c][pl.ds(OFF_MAX + starts[ph], half)] = total.astype(jnp.bfloat16)

        @pl.when(there[ph])
        def _():
            halo(ph, c).start()

    def store(c):
        b, t = divmod(c, 2)
        return pltpu.make_async_copy(result.at[c], out.at[c], out_sem.at[c])

    def compute(c):
        b, t = divmod(c, 2)
        for ph in range(2):

            @pl.when(there[ph])
            def _():
                halo(ph, c).wait_recv()

        lefts = []
        for m in range(modes):
            w, bose = offset[m], occupation[m]
            up, down = (bose + 1.0, bose) if t == 0 else (bose, bose + 1.0)
            plus = ext[c][pl.ds(OFF_MAX + w, e_local)].astype(jnp.float32)
            minus = ext[c][pl.ds(OFF_MAX - w, e_local)].astype(jnp.float32)
            source = (up * plus + down * minus).astype(jnp.bfloat16)
            wide = jnp.concatenate([source[e] for e in range(e_local)], axis=1)
            lefts.append(
                jnp.dot(left_w[b, m], wide, preferred_element_type=jnp.float32).astype(jnp.bfloat16)
            )
        tall = jnp.concatenate(
            [
                jnp.concatenate([x[:, 2 * norb * e : 2 * norb * (e + 1)] for x in lefts], axis=1)
                for e in range(e_local)
            ],
            axis=0,
        )
        total = jnp.dot(tall, right_w[b], preferred_element_type=jnp.float32)
        result[c] = total.astype(jnp.bfloat16).reshape(e_local, norb, 2 * norb)
        store(c).start()

    for c in range(chunks):
        pair_sum(0, c)
    for c in range(chunks):
        pair_sum(1, c)
        if c > 0:
            compute(c - 1)
    compute(chunks - 1)

    for ph in range(2):
        for c in range(chunks):
            for d in range(1, n_mom):
                cross(ph, c, d).wait_send()

        @pl.when(there[ph])
        def _():
            for c in range(chunks):
                halo(ph, c).wait_send()

    for c in range(chunks):
        store(c).wait()


def deliver(made, out, held, get_sem, put_sem):
    chunks = made.shape[0]
    gets = [pltpu.make_async_copy(made.at[c], held.at[c], get_sem.at[c]) for c in range(chunks)]
    for get in gets:
        get.start()
    puts = []
    for c in range(chunks):
        b, t = divmod(c, 2)
        gets[c].wait()
        puts.append(pltpu.make_async_copy(held.at[c], out.at[0, :, b, t], put_sem.at[c]))
        puts[-1].start()
    for put in puts:
        put.wait()


def local(n_mom, n_en, green, pair_index, pair_weight, offset, occupation, vertex, atoms):
    _, e_local, blocks, _, norb, _ = green.shape
    modes = vertex.shape[0]
    chunks = 2 * blocks
    tile = (norb, 2 * norb)
    slots = max(n_mom - 1, 1)
    bf16 = jnp.bfloat16
    hbm = pl.BlockSpec(memory_space=pl.ANY)
    small = (pair_index, pair_weight, offset, occupation, atoms)
    dma = pltpu.SemaphoreType.DMA
    flops = 2 * e_local * chunks * modes * norb * norb * 4 * norb
    made = pl.pallas_call(
        functools.partial(kernel, n_mom, n_en),
        out_shape=jax.ShapeDtypeStruct((chunks, e_local) + tile, bf16),
        in_specs=[hbm] * 7,
        out_specs=hbm,
        scratch_shapes=[pltpu.SMEM(x.shape, x.dtype) for x in small]
        + [
            pltpu.VMEM(green.shape[1:], bf16),
            pltpu.VMEM((slots, chunks, e_local) + tile, bf16),
            pltpu.VMEM(vertex.shape, bf16),
            pltpu.VMEM((blocks, modes, norb, norb), bf16),
            pltpu.VMEM((blocks, 2 * modes * norb, 2 * norb), bf16),
            pltpu.VMEM((chunks, e_local) + tile, bf16),
            dma((2, chunks, slots)),
            dma((2, chunks, slots)),
            dma((2, chunks)),
            dma((2, chunks)),
            dma((2 + len(small),)),
            dma((chunks,)),
        ]
        + [pltpu.VMEM((e_local + 2 * OFF_MAX,) + tile, bf16) for _ in range(chunks)],
        compiler_params=pltpu.CompilerParams(
            collective_id=0, has_side_effects=True, vmem_limit_bytes=60 * 2**20
        ),
        cost_estimate=pl.CostEstimate(
            flops=flops, bytes_accessed=4 * green.size, transcendentals=0
        ),
    )(green, vertex, pair_index, pair_weight, offset, occupation, atoms)
    return pl.pallas_call(
        deliver,
        out_shape=jax.ShapeDtypeStruct(green.shape, bf16),
        in_specs=[hbm],
        out_specs=hbm,
        scratch_shapes=[
            pltpu.VMEM((chunks, e_local) + tile, bf16),
            dma((chunks,)),
            dma((chunks,)),
        ],
        compiler_params=pltpu.CompilerParams(vmem_limit_bytes=60 * 2**20),
    )(made)


def solution(mesh):
    spec = P("mom", "en", None, None, None, None)
    body = functools.partial(local, mesh.shape["mom"], mesh.shape["en"])
    return jax.shard_map(
        body, mesh=mesh, in_specs=(spec,) + (P(),) * 6, out_specs=spec, check_vma=False
    )
```
